32 devices in a mesh: groups: 1, node: 32 (over z, y, x, core).
Axes of the slice: x: 2, y: 2, z: 4, core: 2. Of those that a mesh axis runs over, the one named last changes fastest.
Arguments:
- hidden_states: bfloat16 [4096, 4096], P(('groups', 'node'))
- norm_gain: float32 [4096], replicated, may hold values from 0.5 to 1.5
- expert_ids: int32 [4096, 2], P(('groups', 'node')), may hold values from 0 to 15, all different within a row; in each aligned block of 128 rows (0 to 127, 128 to 255, ...) at most 24 rows name the same one
- gate_weights: float32 [4096, 2], P(('groups', 'node')), may hold values from 0.1 to 0.6
- w_gate: bfloat16 [32, 4096, 384], P('node'), may hold values from -0.09375 to 0.09375
- w_up: bfloat16 [32, 4096, 384], P('node'), may hold values from -0.09375 to 0.09375
- w_down: bfloat16 [32, 384, 4096], P('node'), may hold values from -0.21875 to 0.21875
- kv_pages: bfloat16 [256, 16, 1024], P(('groups', 'node')), may hold values from -6 to 6
- page_table: int32 [256, 2], P(('groups', 'node')), may hold values from 0 to 31, as said below
- kv_lengths: int32 [32], P(('groups', 'node')), may hold values from 1 to 8, 160 in all
Outputs:
- moe_output: bfloat16 [4096, 4096], P(('groups', 'node'))
- decode_pages: bfloat16 [256, 16, 1024], P(('groups', 'node'))
The draws below stay inside these ranges and needn't reach their ends.
Inputs may be any that keep to these rules, and one draw needn't show every extreme that they name: `expert_ids`: each row names 2 different experts. Among the rows of one device no expert is named more than 24 times, and in every draw some expert is named exactly 24 times by the rows of some device. `page_table`: column 0 is a decode device, column 1 a slot below 8. Pages 2i and 2i+1 of a device go to the same decode device; pages of one device with different i go to different decode devices; for each i, different devices send their pages 2i and 2i+1 to different decode devices; no decode slot is named by two pages. The live pages of device s are its first kv_lengths[s] pages.
All inputs are finite; a program needn't handle non-finite values.
Results may differ from the reference program's by a relative error of at most 0.0077.
Values may be sent and summed in bfloat16 or wider, within the bound.
A program may use at most 128 MiB of HBM per device.

```python
import math
import jax
import jax.numpy as jnp
import numpy as np
from jax import lax

D = 4096
HALF = 384
FF = 768
TOK_DEV = 128
TOKENS = 4096
EXPERTS = 16
TOP = 2
CAP = 24
PAGE = 16
PAGES_DEV = 8
PAGES = 256
KVW = 1024
KV_TOTAL = 160
N_NODE = 32


def draw_hidden_states(key, part):
    key = jax.random.fold_in(key, 11)
    first, second, third = jax.random.split(key, 3)
    base = jax.random.normal(first, (TOKENS, D), jnp.float32)
    column_scale = jnp.exp(jax.random.uniform(second, (1, D), jnp.float32, 0.0, jnp.log(10.0)))
    row_scale = jnp.exp(jax.random.uniform(third, (TOKENS, 1), jnp.float32, 0.0, jnp.log(10.0)))
    return (0.3 * base * column_scale * row_scale).astype(jnp.bfloat16)


def draw_page_table(key, part):
    key = jax.random.fold_in(key, 23)
    first, second, third = jax.random.split(key, 3)
    relabel = jax.random.permutation(first, N_NODE).astype(jnp.int32)
    shifts = jax.random.permutation(second, N_NODE).astype(jnp.int32)[:PAGES_DEV // 2]
    slot_order = jax.random.permutation(third, PAGES_DEV).astype(jnp.int32)
    source = jnp.arange(N_NODE, dtype=jnp.int32)[:, None]
    pair_index = jnp.arange(PAGES_DEV, dtype=jnp.int32)[None, :] // 2
    destination = (relabel[source] + shifts[pair_index]) % N_NODE
    slot_index = jnp.broadcast_to(slot_order[None, :], (N_NODE, PAGES_DEV))
    return jnp.stack([destination, slot_index], axis=-1).reshape(PAGES, 2).astype(jnp.int32)


def shard_levels(rng, extent, shards, least, top_value):
    def one(position, parts):
        heights = jax.random.uniform(jax.random.fold_in(jax.random.fold_in(rng, 6), position), (parts,), jnp.float32, least / len(shards), top_value / len(shards))
        return jnp.repeat(jnp.exp(heights), extent[position] // parts).reshape((-1,) + (1,) * (len(extent) - position - 1))

    factor_of = one(*shards[0])
    for cut in shards[1:]:
        factor_of = factor_of * one(*cut)
    return factor_of


def profile(count, total, limit, slope):
    portions = [(1 << 20) // math.isqrt(rank ** slope) + 1 for rank in range(2, count + 1)]
    rest, given = total - limit - (count - 1), [1] * (count - 1)
    while rest > 0:
        movable = [i for i in range(count - 1) if given[i] < limit]
        pool, remaining = sum([portions[i] for i in movable]), rest
        for i in movable:
            addition = min(limit - given[i], max(1, remaining * portions[i] // pool), rest)
            given[i] = given[i] + addition
            rest = rest - addition
    return np.array([limit] + given)


def uneven_parts(stream_key, amount, total, limit, lean):
    if amount == 2:
        one = jax.random.randint(stream_key, (), max(1, total - limit), min(limit, total - 1) + 1)
        return jnp.stack([one, total - one])
    lengths = jnp.asarray(profile(amount, total, limit, lean), jnp.int32)
    pairs = (amount - 1) // 2
    donor, sink = lengths[1:1 + 2 * pairs:2], lengths[2:2 + 2 * pairs:2]
    slack = jnp.minimum(donor - 1, limit - sink)
    shifted = jax.random.randint(jax.random.fold_in(stream_key, 1), (pairs,), 0, 1 << 20) % (slack + 1)
    lengths = lengths.at[1:1 + 2 * pairs:2].set(donor - shifted).at[2:2 + 2 * pairs:2].set(sink + shifted)
    return lengths[jax.random.permutation(jax.random.fold_in(stream_key, 2), amount)]


def deal_out(rng, own, number, rows, amount, top, most, lean):
    order = jax.random.permutation(rng, amount)
    crowded, usual = portions_of(amount, rows * top, most, lean, True), portions_of(amount, rows * top, most, lean, False)
    places = jnp.arange(amount)

    def named(sizes, turn):
        used = int((sizes > 0).sum())
        fixed = max(1, used // 4)
        shifted = fixed + (places - fixed + turn * (used - fixed)) % max(1, amount - fixed)
        return jnp.zeros((amount,), jnp.int32).at[order[jnp.where(places < fixed, places, shifted)]].set(jnp.asarray(sizes, jnp.int32))

    sizes = jnp.where(number % 4 == 0, named(crowded, number // 4), named(usual, number - number // 4 - 1))
    mixed = jax.random.permutation(jax.random.fold_in(own, 3), amount)
    donor, taker = mixed[0:amount // 2 * 2:2], mixed[1:amount // 2 * 2:2]
    margin = jnp.minimum(sizes[donor] - 1, most - sizes[taker]) // 2
    margin = jnp.where((donor == order[0]) | (taker == order[0]) | (sizes[taker] == 0), 0, jnp.maximum(margin, 0))
    shifted = jax.random.randint(jax.random.fold_in(own, 4), (amount // 2,), 0, 1 << 20) % (margin + 1)
    sizes = sizes.at[donor].add(-shifted).at[taker].add(shifted)
    items = jnp.searchsorted(jnp.cumsum(sizes), jnp.arange(rows * top), side="right").astype(jnp.int32)
    grid = items.reshape(top, rows).T
    grid = grid[jax.random.permutation(jax.random.fold_in(own, 1), rows)]
    turn = jax.random.randint(jax.random.fold_in(own, 2), (rows, 1), 0, top)
    return jnp.take_along_axis(grid, (jnp.arange(top)[None, :] + turn) % top, axis=1)


def portions_of(count, total, reach, slope, full):
    loads = [(1 << 20) // math.isqrt(grade ** slope) + 1 for grade in range(1, count + 1)]
    largest = reach if full else min(reach, max(-(-total // count), total * loads[0] // sum(loads)))
    least = 1 if total - largest >= count - 1 else 0
    given, spare = [largest] + [least] * (count - 1), total - largest - least * (count - 1)
    while spare > 0:
        movable = [i for i in range(1, count) if given[i] < largest] or [i for i in range(1, count) if given[i] < reach]
        mass, left = sum([loads[i] for i in movable]), spare
        for i in movable:
            more = min(reach - given[i], max(1, left * loads[i] // mass), spare)
            given[i] = given[i] + more
            spare = spare - more
    return np.array(given)


def bell_draw(stream_key, dims, width, most, cuts=(), held_as=jnp.bfloat16):
    array = jax.random.normal(stream_key, dims, jnp.float32) * width
    if len(cuts) > 0:
        array = shard_levels(stream_key, dims, cuts, -0.22, 0.18) * array
    return jnp.clip(array, min=-most, max=most).astype(held_as)


def setup_inputs(seed: int = 0, part: int = 0) -> dict:
    keys = jax.random.split(jax.random.key(seed), 11)
    part_keys = jax.random.split(jax.random.fold_in(keys[10], part), 11)
    hidden_states = draw_hidden_states(jax.random.fold_in(jax.random.fold_in(keys[10], part), 71), part)
    norm_gain = jnp.clip(1.0 + 0.1 * jax.random.normal(keys[1], (D,), jnp.float32), 0.5, 1.5)
    expert_ids_keys = jax.random.split(jax.random.fold_in(part_keys[2], 1), TOKENS // TOK_DEV)
    expert_ids_turns = jax.random.permutation(jax.random.fold_in(part_keys[2], 3), TOKENS // TOK_DEV)
    expert_ids = jax.vmap(lambda own, number: deal_out(jax.random.fold_in(part_keys[2], 2), own, number, TOK_DEV, EXPERTS, TOP, CAP, 2))(expert_ids_keys, expert_ids_turns).reshape((TOKENS, TOP))
    gate_weights = jnp.clip(0.1 + 0.5 * jax.random.uniform(part_keys[3], (TOKENS, TOP), jnp.float32) ** shard_levels(part_keys[3], (TOKENS, TOP), ((0, 32),), -0.2, 0.2), 0.1, 0.6)
    w_gate = bell_draw(keys[4], (2 * EXPERTS, D, HALF), D ** -0.5, 0.09375, ((0, 32),))
    w_up = bell_draw(keys[5], (2 * EXPERTS, D, HALF), D ** -0.5, 0.09375, ((0, 32),))
    w_down = bell_draw(keys[6], (2 * EXPERTS, HALF, D), FF ** -0.5, 0.21875, ((0, 32),))
    kv_pages = bell_draw(part_keys[7], (PAGES, PAGE, KVW), 1.0, 6.0, ((0, 32),))
    page_table = draw_page_table(jax.random.fold_in(jax.random.fold_in(keys[10], part), 71), part)
    kv_lengths = uneven_parts(part_keys[9], N_NODE, KV_TOTAL, PAGES_DEV, 2).astype(jnp.int32)
    return {"hidden_states": hidden_states, "norm_gain": norm_gain, "expert_ids": expert_ids, "gate_weights": gate_weights, "w_gate": w_gate, "w_up": w_up, "w_down": w_down, "kv_pages": kv_pages, "page_table": page_table, "kv_lengths": kv_lengths}


def reference(hidden_states, norm_gain, expert_ids, gate_weights, w_gate, w_up, w_down, kv_pages, page_table, kv_lengths):
    values = hidden_states.astype(jnp.float32)
    factor = lax.rsqrt(lax.optimization_barrier(jnp.mean(values * values, axis=1, keepdims=True)) + 1e-06)
    normed = (values * factor * norm_gain[None, :]).astype(jnp.bfloat16)
    grouped_ids = expert_ids.reshape(N_NODE, TOK_DEV * TOP)
    onehot = (grouped_ids[:, :, None] == jnp.arange(EXPERTS, dtype=jnp.int32)[None, None, :]).astype(jnp.int32)
    rank_index = lax.optimization_barrier(jnp.sum((jnp.cumsum(onehot, axis=1) - onehot) * onehot, axis=2))
    source = jnp.arange(N_NODE, dtype=jnp.int32)[:, None]
    row_index = (source * CAP + rank_index).reshape(TOKENS, TOP).astype(jnp.int32)

    def one_expert(expert):
        row_block = jnp.zeros((N_NODE * CAP, D), jnp.bfloat16)
        for pick_index in range(TOP):
            target = jnp.where(expert_ids[:, pick_index] == expert, row_index[:, pick_index], N_NODE * CAP)
            row_block = row_block.at[target].set(normed, mode='drop')
        gate_full = jnp.concatenate([w_gate[2 * expert], w_gate[2 * expert + 1]], axis=1)
        up_full = jnp.concatenate([w_up[2 * expert], w_up[2 * expert + 1]], axis=1)
        gate_sum = jnp.dot(row_block, gate_full, preferred_element_type=jnp.float32)
        up_sum = jnp.dot(row_block, up_full, preferred_element_type=jnp.float32)
        activated = (jax.nn.silu(gate_sum) * up_sum).astype(jnp.bfloat16)
        first_part = jnp.dot(activated[:, :HALF], w_down[2 * expert], preferred_element_type=jnp.float32).astype(jnp.bfloat16)
        second_part = jnp.dot(activated[:, HALF:], w_down[2 * expert + 1], preferred_element_type=jnp.float32).astype(jnp.bfloat16)
        return (first_part.astype(jnp.float32) + second_part.astype(jnp.float32)).astype(jnp.bfloat16)
    outputs = lax.map(one_expert, jnp.arange(EXPERTS, dtype=jnp.int32))
    picked = outputs[expert_ids, row_index]
    moe_output = lax.optimization_barrier(jnp.sum(gate_weights[:, :, None] * picked.astype(jnp.float32), axis=1)).astype(jnp.bfloat16)
    is_live = (jnp.arange(PAGES_DEV, dtype=jnp.int32)[None, :] < kv_lengths[:, None]).reshape(PAGES)
    flat_index = page_table[:, 0] * PAGES_DEV + page_table[:, 1]
    target_page = jnp.where(is_live, flat_index, PAGES).astype(jnp.int32)
    decode_pages = jnp.zeros((PAGES, PAGE, KVW), jnp.bfloat16).at[target_page].set(kv_pages, mode='drop')
    return (moe_output, decode_pages)
```

```python
import jax
import jax.numpy as jnp
from jax import lax
from jax.sharding import PartitionSpec as P

BF = jnp.bfloat16
F32 = jnp.float32


def dot32(a, b):
    return jnp.dot(a, b, preferred_element_type=F32)


def all_to_all(x):
    return lax.all_to_all(x, "node", split_axis=0, concat_axis=0, tiled=True)


def pages_phase_one(kv_pages, page_table, kv_lengths, nodes):
    pages_dev, page_len, kv_width = kv_pages.shape
    piece = page_len * kv_width // nodes
    live = jnp.arange(pages_dev, dtype=jnp.int32) < kv_lengths[0]
    code = jnp.where(live, page_table[:, 0] * pages_dev + page_table[:, 1], -1)
    codes = lax.all_gather(code, "node", axis=0, tiled=True)
    pieces = kv_pages.reshape(pages_dev, nodes, piece).swapaxes(0, 1)
    return codes, all_to_all(pieces).reshape(nodes * pages_dev, piece)


def pages_phase_two(codes, pieces, nodes, shape):
    pages_dev = shape[0]
    placing = (codes[None, :] == jnp.arange(codes.shape[0], dtype=jnp.int32)[:, None]).astype(BF)
    sent = dot32(placing, pieces).astype(BF).reshape(nodes, pages_dev, -1)
    return all_to_all(sent).swapaxes(0, 1).reshape(shape)


def shards(
    hidden_states,
    norm_gain,
    expert_ids,
    gate_weights,
    w_gate,
    w_up,
    w_down,
    kv_pages,
    page_table,
    kv_lengths,
):
    nodes = lax.axis_size("node")
    experts = nodes // 2
    core = lax.axis_index("node") % 2
    tok_rows, width = hidden_states.shape
    half = width // 2
    top = expert_ids.shape[1]
    cap = tok_rows * top * 3 // (2 * experts)
    rows = nodes * cap

    codes, pieces = pages_phase_one(kv_pages, page_table, kv_lengths, nodes)

    flat = expert_ids.reshape(-1)
    pairs = flat.shape[0]
    onehot = flat[:, None] == jnp.arange(experts, dtype=jnp.int32)[None, :]
    steps = jnp.arange(pairs, dtype=jnp.int32)
    before = dot32((steps[:, None] > steps[None, :]).astype(BF), onehot.astype(BF))
    rank = jnp.sum(jnp.where(onehot, before, 0.0), axis=1).astype(jnp.int32)
    slot = (flat * (2 * cap) + rank).reshape(tok_rows, top)
    places = jnp.arange(rows, dtype=jnp.int32)

    values = hidden_states.astype(F32)
    factor = lax.rsqrt(jnp.mean(values * values, axis=1, keepdims=True) + 1e-06)
    normed = (values * factor * norm_gain[None, :]).astype(BF)

    def hits(shift):
        return slot[:, :, None] + shift == places[None, None, :]

    placed = jnp.concatenate(
        [jnp.any(hits(0), axis=1), jnp.any(hits(cap), axis=1)], axis=0
    ).astype(BF)
    stacked = jnp.concatenate([normed[:, :half], normed[:, half:]], axis=0)
    outgoing = lax.dot_general(
        placed, stacked, (((0,), (0,)), ((), ())), preferred_element_type=F32
    ).astype(BF)
    mine = all_to_all(outgoing.reshape(nodes, cap, half)).reshape(rows, half)

    swap = [(i, i ^ 1) for i in range(nodes)]
    other = lax.ppermute(mine, "node", swap)
    here, there = core * half, (1 - core) * half

    def halves(w, start, axis):
        return lax.dynamic_slice_in_dim(w, start, half, axis)

    gate = dot32(mine, halves(w_gate[0], here, 0)) + dot32(other, halves(w_gate[0], there, 0))
    up = dot32(mine, halves(w_up[0], here, 0)) + dot32(other, halves(w_up[0], there, 0))
    activated = (jax.nn.silu(gate) * up).astype(BF)
    away = dot32(activated, halves(w_down[0], there, 1)).astype(BF)
    arrived = lax.ppermute(away, "node", swap)
    summed = (dot32(activated, halves(w_down[0], here, 1)) + arrived.astype(F32)).astype(BF)
    returned = all_to_all(summed.reshape(nodes, cap, half)).reshape(rows, half)

    def weights(shift):
        return jnp.sum(jnp.where(hits(shift), gate_weights[:, :, None], 0.0), axis=1)

    scale = jnp.concatenate([weights(0), weights(cap)], axis=0)
    high = scale.astype(BF)
    low = (scale - high.astype(F32)).astype(BF)
    mixed = (dot32(high, returned) + dot32(low, returned)).astype(BF)
    moe_output = jnp.concatenate([mixed[:tok_rows], mixed[tok_rows:]], axis=1)
    decode_pages = pages_phase_two(codes, pieces, nodes, kv_pages.shape)
    return (moe_output, decode_pages)


def solution(mesh):
    placed = (
        P(("groups", "node"), None),
        P(),
        P(("groups", "node"), None),
        P(("groups", "node"), None),
        P("node", None, None),
        P("node", None, None),
        P("node", None, None),
        P(("groups", "node"), None, None),
        P(("groups", "node"), None),
        P(("groups", "node")),
    )
    return jax.shard_map(
        shards,
        mesh=mesh,
        in_specs=placed,
        out_specs=(P(("groups", "node"), None), P(("groups", "node"), None, None)),
        check_vma=False,
    )
```

```python
import jax
import jax.numpy as jnp
from jax import lax
from jax.sharding import PartitionSpec as P

BF = jnp.bfloat16
F32 = jnp.float32


def dot32(a, b):
    return jnp.dot(a, b, preferred_element_type=F32)


def all_to_all(x):
    return lax.all_to_all(x, "node", split_axis=0, concat_axis=0, tiled=True)


def pages_phase_one(kv_pages, page_table, kv_lengths, nodes):
    pages_dev, page_len, kv_width = kv_pages.shape
    piece = page_len * kv_width // nodes
    live = jnp.arange(pages_dev, dtype=jnp.int32) < kv_lengths[0]
    marks = jnp.stack([jnp.where(live, page_table[:, 0], -1), page_table[:, 1]], axis=1).astype(BF)
    tail = jnp.broadcast_to(jnp.pad(marks, ((0, 0), (0, 126)))[None], (nodes, pages_dev, 128))
    pieces = kv_pages.reshape(pages_dev, nodes, piece).swapaxes(0, 1)
    sent = jnp.concatenate([pieces, tail], axis=2)
    return all_to_all(sent).reshape(nodes * pages_dev, piece + 128)


def pages_phase_two(got, nodes, shape):
    pages_dev = shape[0]
    piece = got.shape[1] - 128
    marks = got[:, piece : piece + 2].astype(jnp.int32)
    code = jnp.where(marks[:, 0] < 0, -1, marks[:, 0] * pages_dev + marks[:, 1])
    placing = (code[None, :] == jnp.arange(code.shape[0], dtype=jnp.int32)[:, None]).astype(BF)
    sent = dot32(placing, got[:, :piece]).astype(BF).reshape(nodes, pages_dev, piece)
    return all_to_all(sent)


def shards(
    hidden_states,
    norm_gain,
    expert_ids,
    gate_weights,
    w_gate,
    w_up,
    w_down,
    kv_pages,
    page_table,
    kv_lengths,
):
    nodes = lax.axis_size("node")
    experts = nodes // 2
    core = lax.axis_index("node") % 2
    tok_rows, width = hidden_states.shape
    half = width // 2
    top = expert_ids.shape[1]
    cap = tok_rows * top * 3 // (2 * experts)
    rows = nodes * cap

    page_pieces = pages_phase_one(kv_pages, page_table, kv_lengths, nodes)

    flat = expert_ids.reshape(-1)
    pairs = flat.shape[0]
    onehot = flat[:, None] == jnp.arange(experts, dtype=jnp.int32)[None, :]
    steps = jnp.arange(pairs, dtype=jnp.int32)
    before = dot32((steps[:, None] > steps[None, :]).astype(BF), onehot.astype(BF))
    rank = jnp.sum(jnp.where(onehot, before, 0.0), axis=1).astype(jnp.int32)
    ids = expert_ids[:, :, None]
    rank = rank.reshape(tok_rows, top, 1)
    values = hidden_states.astype(F32)
    factor = lax.rsqrt(jnp.mean(values * values, axis=1, keepdims=True) + 1e-06)
    normed = (values * factor * norm_gain[None, :]).astype(BF)

    stacked = jnp.concatenate([normed[:, :half], normed[:, half:]], axis=0)
    swap = [(i, i ^ 1) for i in range(nodes)]
    here, there = core * half, (1 - core) * half

    def halves(w, start, axis):
        return lax.dynamic_slice_in_dim(w, start, half, axis)

    gate_here, gate_there = halves(w_gate[0], here, 0), halves(w_gate[0], there, 0)
    up_here, up_there = halves(w_up[0], here, 0), halves(w_up[0], there, 0)
    down_here, down_there = halves(w_down[0], here, 1), halves(w_down[0], there, 1)

    def hits(first, count, second):
        inside = (rank >= first) & (rank < first + count)
        slot = jnp.where(inside, (ids * 2 + second) * count + rank - first, -1)
        return slot == jnp.arange(nodes * count, dtype=jnp.int32)[None, None, :]

    def send(first, count):
        placed = jnp.concatenate(
            [jnp.any(hits(first, count, c), axis=1) for c in (0, 1)], axis=0
        ).astype(BF)
        return lax.dot_general(
            placed, stacked, (((0,), (0,)), ((), ())), preferred_element_type=F32
        ).astype(BF).reshape(nodes, count, half)

    def expert(mine):
        other = lax.ppermute(mine, "node", swap)
        gate = dot32(mine, gate_here) + dot32(other, gate_there)
        up = dot32(mine, up_here) + dot32(other, up_there)
        activated = (jax.nn.silu(gate) * up).astype(BF)
        arrived = lax.ppermute(dot32(activated, down_there).astype(BF), "node", swap)
        return (dot32(activated, down_here) + arrived.astype(F32)).astype(BF)

    def combine(first, count, returned):
        scale = jnp.concatenate(
            [
                jnp.sum(jnp.where(hits(first, count, c), gate_weights[:, :, None], 0.0), axis=1)
                for c in (0, 1)
            ],
            axis=0,
        )
        high = scale.astype(BF)
        low = (scale - high.astype(F32)).astype(BF)
        return dot32(high, returned) + dot32(low, returned)

    large = cap * 2 // 3
    small = cap - large
    one = all_to_all(send(0, large)).reshape(nodes * large, half)
    two_out, one = lax.optimization_barrier((send(large, small), one))
    two = all_to_all(two_out).reshape(nodes * small, half)
    one_done = expert(one)
    slots = pages_phase_two(page_pieces, nodes, kv_pages.shape)
    one_done, two = lax.optimization_barrier((one_done, two))
    one_back = all_to_all(one_done.reshape(nodes, large, half)).reshape(nodes * large, half)
    two_done = expert(two)
    two_done, one_back = lax.optimization_barrier((two_done, one_back))
    two_back = all_to_all(two_done.reshape(nodes, small, half)).reshape(nodes * small, half)
    mixed = (combine(0, large, one_back) + combine(large, small, two_back)).astype(BF)
    moe_output = jnp.concatenate([mixed[:tok_rows], mixed[tok_rows:]], axis=1)
    return (moe_output, slots.swapaxes(0, 1).reshape(kv_pages.shape))


def solution(mesh):
    placed = (
        P(("groups", "node"), None),
        P(),
        P(("groups", "node"), None),
        P(("groups", "node"), None),
        P("node", None, None),
        P("node", None, None),
        P("node", None, None),
        P(("groups", "node"), None, None),
        P(("groups", "node"), None),
        P(("groups", "node")),
    )
    return jax.shard_map(
        shards,
        mesh=mesh,
        in_specs=placed,
        out_specs=(P(("groups", "node"), None), P(("groups", "node"), None, None)),
        check_vma=False,
    )
```

```python
import jax
import jax.numpy as jnp
from jax import lax
from jax.sharding import PartitionSpec as P

BF = jnp.bfloat16
F32 = jnp.float32


def dot32(a, b):
    return jnp.dot(a, b, preferred_element_type=F32)


def all_to_all(x, groups=None):
    return lax.all_to_all(
        x, "node", split_axis=0, concat_axis=0, axis_index_groups=groups, tiled=True
    )


def pages_phase_one(kv_pages, page_table, kv_lengths, nodes):
    pages_dev, page_len, kv_width = kv_pages.shape
    piece = page_len * kv_width // nodes
    live = jnp.arange(pages_dev, dtype=jnp.int32) < kv_lengths[0]
    marks = jnp.stack([jnp.where(live, page_table[:, 0], -1), page_table[:, 1]], axis=1).astype(BF)
    tail = jnp.broadcast_to(jnp.pad(marks, ((0, 0), (0, 126)))[None], (nodes, pages_dev, 128))
    pieces = kv_pages.reshape(pages_dev, nodes, piece).swapaxes(0, 1)
    sent = jnp.concatenate([pieces, tail], axis=2)
    return all_to_all(sent).reshape(nodes * pages_dev, piece + 128)


def pages_phase_two(got, nodes, shape):
    pages_dev = shape[0]
    piece = got.shape[1] - 128
    marks = got[:, piece : piece + 2].astype(jnp.int32)
    code = jnp.where(marks[:, 0] < 0, -1, marks[:, 0] * pages_dev + marks[:, 1])
    placing = (code[None, :] == jnp.arange(code.shape[0], dtype=jnp.int32)[:, None]).astype(BF)
    sent = dot32(placing, got[:, :piece]).astype(BF).reshape(nodes, pages_dev, piece)
    return all_to_all(sent)


def shards(
    hidden_states,
    norm_gain,
    expert_ids,
    gate_weights,
    w_gate,
    w_up,
    w_down,
    kv_pages,
    page_table,
    kv_lengths,
):
    nodes = lax.axis_size("node")
    experts = nodes // 2
    tok_rows, width = hidden_states.shape
    top = expert_ids.shape[1]
    cap = tok_rows * top * 3 // (2 * experts)

    page_pieces = pages_phase_one(kv_pages, page_table, kv_lengths, nodes)

    flat = expert_ids.reshape(-1)
    pairs = flat.shape[0]
    onehot = flat[:, None] == jnp.arange(experts, dtype=jnp.int32)[None, :]
    steps = jnp.arange(pairs, dtype=jnp.int32)
    before = dot32((steps[:, None] > steps[None, :]).astype(BF), onehot.astype(BF))
    rank = jnp.sum(jnp.where(onehot, before, 0.0), axis=1).astype(jnp.int32)
    ids = expert_ids[:, :, None]
    rank = rank.reshape(tok_rows, top, 1)
    values = hidden_states.astype(F32)
    factor = lax.rsqrt(jnp.mean(values * values, axis=1, keepdims=True) + 1e-06)
    normed = (values * factor * norm_gain[None, :]).astype(BF)

    swap = [(i, i ^ 1) for i in range(nodes)]
    parity = [list(range(c, nodes, 2)) for c in (0, 1)]

    def both(w):
        return w[0], lax.ppermute(w, "node", swap)[0]

    weights = list(zip(both(w_gate), both(w_up), both(w_down)))

    def hits(first, count):
        inside = (rank >= first) & (rank < first + count)
        slot = jnp.where(inside, ids * count + rank - first, -1)
        return slot == jnp.arange(experts * count, dtype=jnp.int32)[None, None, :]

    def send(first, count):
        placed = jnp.any(hits(first, count), axis=1).astype(BF)
        rows = lax.dot_general(
            placed, normed, (((0,), (0,)), ((), ())), preferred_element_type=F32
        )
        return rows.astype(BF).reshape(experts, count, width)

    def exchange(x):
        return all_to_all(x.reshape(experts, -1, width), parity).reshape(-1, width)

    def expert(x):
        total = None
        for gate_w, up_w, down_w in weights:
            activated = (jax.nn.silu(dot32(x, gate_w)) * dot32(x, up_w)).astype(BF)
            part = dot32(activated, down_w)
            total = part if total is None else total + part
        return total.astype(BF)

    def combine(first, count, returned):
        scale = jnp.sum(jnp.where(hits(first, count), gate_weights[:, :, None], 0.0), axis=1)
        high = scale.astype(BF)
        low = (scale - high.astype(F32)).astype(BF)
        return dot32(high, returned) + dot32(low, returned)

    large = cap * 2 // 3
    small = cap - large
    one_out, page_pieces = lax.optimization_barrier((send(0, large), page_pieces))
    one = exchange(one_out)
    two_out, one = lax.optimization_barrier((send(large, small), one))
    two = exchange(two_out)
    one_done = expert(one)
    slots = pages_phase_two(page_pieces, nodes, kv_pages.shape)
    one_done, two = lax.optimization_barrier((one_done, two))
    one_back = exchange(one_done)
    two_done = expert(two)
    two_done, one_back = lax.optimization_barrier((two_done, one_back))
    two_back = exchange(two_done)
    moe_output = (combine(0, large, one_back) + combine(large, small, two_back)).astype(BF)
    return (moe_output, slots.swapaxes(0, 1).reshape(kv_pages.shape))


def solution(mesh):
    placed = (
        P(("groups", "node"), None),
        P(),
        P(("groups", "node"), None),
        P(("groups", "node"), None),
        P("node", None, None),
        P("node", None, None),
        P("node", None, None),
        P(("groups", "node"), None, None),
        P(("groups", "node"), None),
        P(("groups", "node")),
    )
    return jax.shard_map(
        shards,
        mesh=mesh,
        in_specs=placed,
        out_specs=(P(("groups", "node"), None), P(("groups", "node"), None, None)),
        check_vma=False,
    )
```

```python
import jax
import jax.numpy as jnp
from jax import lax
from jax.sharding import PartitionSpec as P

BF = jnp.bfloat16
F32 = jnp.float32


def dot32(a, b):
    return jnp.dot(a, b, preferred_element_type=F32)


def all_to_all(x, groups=None):
    return lax.all_to_all(
        x, "node", split_axis=0, concat_axis=0, axis_index_groups=groups, tiled=True
    )


def by_core(core, pair):
    first, second = pair
    return jnp.where(core == 0, first, second), jnp.where(core == 0, second, first)


def pages_out(kv_pages, page_table, kv_lengths, core, swap, chips, rows):
    pages_dev, page_len, kv_width = kv_pages.shape
    live = jnp.arange(pages_dev, dtype=jnp.int32) < kv_lengths[0]
    marks = jnp.stack([jnp.where(live, page_table[:, 0], -1), page_table[:, 1]], axis=1)
    marks = jnp.concatenate([marks, lax.ppermute(marks, "node", swap)], axis=0)
    split = kv_pages.reshape(pages_dev, chips, 2, -1)
    keep, give = by_core(core, (split[:, :, 0], split[:, :, 1]))
    pieces = jnp.concatenate([keep, lax.ppermute(give, "node", swap)], axis=0).swapaxes(0, 1)
    tail = jnp.pad(marks.reshape(-1).astype(BF), (0, 128 - marks.size))
    tail = jnp.broadcast_to(tail[None, None, :], (chips, rows, 128))
    return jnp.concatenate([pieces.reshape(chips, rows, -1), tail], axis=2)


def pages_place(got, pages_dev, chips, rows):
    count = 2 * pages_dev
    pieces = got[:, :, :-128].reshape(chips * count, -1)
    marks = got[:, 0, -128:][:, : 2 * count].astype(jnp.int32).reshape(chips * count, 2)
    code = jnp.where(marks[:, 0] < 0, -1, marks[:, 0] * pages_dev + marks[:, 1])
    placing = (code[None, :] == jnp.arange(code.shape[0], dtype=jnp.int32)[:, None]).astype(BF)
    return dot32(placing, pieces).astype(BF).reshape(chips, rows, -1)


def pages_in(got, core, swap, shape):
    pages_dev = shape[0]
    got = got.reshape(got.shape[0], 2 * pages_dev, -1)
    keep, give = by_core(core, (got[:, :pages_dev], got[:, pages_dev:]))
    pair = by_core(core, (keep, lax.ppermute(give, "node", swap)))
    return jnp.stack(pair, axis=1).transpose(2, 0, 1, 3).reshape(shape)


def shards(
    hidden_states,
    norm_gain,
    expert_ids,
    gate_weights,
    w_gate,
    w_up,
    w_down,
    kv_pages,
    page_table,
    kv_lengths,
):
    nodes = lax.axis_size("node")
    experts = nodes // 2
    tok_rows, width = hidden_states.shape
    top = expert_ids.shape[1]
    cap = tok_rows * top * 3 // (2 * experts)

    core = lax.axis_index("node") % 2
    swap = [(i, i ^ 1) for i in range(nodes)]
    pages_dev = kv_pages.shape[0]
    large = cap * 2 // 3
    small = cap - large

    flat = expert_ids.reshape(-1)
    pairs = flat.shape[0]
    onehot = flat[:, None] == jnp.arange(experts, dtype=jnp.int32)[None, :]
    steps = jnp.arange(pairs, dtype=jnp.int32)
    before = dot32((steps[:, None] > steps[None, :]).astype(BF), onehot.astype(BF))
    rank = jnp.sum(jnp.where(onehot, before, 0.0), axis=1).astype(jnp.int32)
    ids = expert_ids[:, :, None]
    rank = rank.reshape(tok_rows, top, 1)
    values = hidden_states.astype(F32)
    factor = lax.rsqrt(jnp.mean(values * values, axis=1, keepdims=True) + 1e-06)
    normed = (values * factor * norm_gain[None, :]).astype(BF)

    parity = [list(range(c, nodes, 2)) for c in (0, 1)]

    def both(w):
        return w[0], lax.ppermute(w, "node", swap)[0]

    weights = list(zip(both(w_gate), both(w_up), both(w_down)))

    def hits(first, count):
        inside = (rank >= first) & (rank < first + count)
        slot = jnp.where(inside, ids * count + rank - first, -1)
        return slot == jnp.arange(experts * count, dtype=jnp.int32)[None, None, :]

    def send(first, count):
        placed = jnp.any(hits(first, count), axis=1).astype(BF)
        rows = lax.dot_general(
            placed, normed, (((0,), (0,)), ((), ())), preferred_element_type=F32
        )
        return rows.astype(BF).reshape(experts, count, width)

    def exchange(x):
        return all_to_all(x, parity)

    def expert(x):
        total = None
        for gate_w, up_w, down_w in weights:
            activated = (jax.nn.silu(dot32(x, gate_w)) * dot32(x, up_w)).astype(BF)
            part = dot32(activated, down_w)
            total = part if total is None else total + part
        return total.astype(BF)

    def combine(first, count, returned):
        scale = jnp.sum(jnp.where(hits(first, count), gate_weights[:, :, None], 0.0), axis=1)
        high = scale.astype(BF)
        low = (scale - high.astype(F32)).astype(BF)
        return dot32(high, returned) + dot32(low, returned)

    one = exchange(send(0, large)).reshape(-1, width)
    pages = pages_out(kv_pages, page_table, kv_lengths, core, swap, experts, small)
    two_out = jnp.concatenate([send(large, small), pages], axis=2)
    two_out, one = lax.optimization_barrier((two_out, one))
    two = exchange(two_out)
    one_done = expert(one).reshape(experts, large, width)
    slots = pages_place(two[:, :, width:], pages_dev, experts, large)
    two = two[:, :, :width].reshape(-1, width)
    one_back = exchange(jnp.concatenate([one_done, slots], axis=2))
    two_done = expert(two).reshape(experts, small, width)
    two_done, one_back = lax.optimization_barrier((two_done, one_back))
    two_back = exchange(two_done).reshape(-1, width)
    decode_pages = pages_in(one_back[:, :, width:], core, swap, kv_pages.shape)
    one_back = one_back[:, :, :width].reshape(-1, width)
    moe_output = (combine(0, large, one_back) + combine(large, small, two_back)).astype(BF)
    return (moe_output, decode_pages)


def solution(mesh):
    placed = (
        P(("groups", "node"), None),
        P(),
        P(("groups", "node"), None),
        P(("groups", "node"), None),
        P("node", None, None),
        P("node", None, None),
        P("node", None, None),
        P(("groups", "node"), None, None),
        P(("groups", "node"), None),
        P(("groups", "node")),
    )
    return jax.shard_map(
        shards,
        mesh=mesh,
        in_specs=placed,
        out_specs=(P(("groups", "node"), None), P(("groups", "node"), None, None)),
        check_vma=False,
    )
```

```python
import jax
import jax.numpy as jnp
from jax import lax
from jax.sharding import PartitionSpec as P

BF = jnp.bfloat16
F32 = jnp.float32


def dot32(a, b):
    return jnp.dot(a, b, preferred_element_type=F32)


def all_to_all(x, groups=None):
    return lax.all_to_all(
        x, "node", split_axis=0, concat_axis=0, axis_index_groups=groups, tiled=True
    )


def by_core(core, pair):
    first, second = pair
    return jnp.where(core == 0, first, second), jnp.where(core == 0, second, first)


def pages_out(kv_pages, page_table, kv_lengths, core, swap, chips, rows):
    pages_dev, page_len, kv_width = kv_pages.shape
    live = jnp.arange(pages_dev, dtype=jnp.int32) < kv_lengths[0]
    marks = jnp.stack([jnp.where(live, page_table[:, 0], -1), page_table[:, 1]], axis=1)
    marks = jnp.concatenate([marks, lax.ppermute(marks, "node", swap)], axis=0)
    split = kv_pages.reshape(pages_dev, chips, 2, -1)
    keep, give = by_core(core, (split[:, :, 0], split[:, :, 1]))
    pieces = jnp.concatenate([keep, lax.ppermute(give, "node", swap)], axis=0).swapaxes(0, 1)
    tail = jnp.pad(marks.reshape(-1).astype(BF), (0, 128 - marks.size))
    tail = jnp.broadcast_to(tail[None, None, :], (chips, rows, 128))
    return jnp.concatenate([pieces.reshape(chips, rows, -1), tail], axis=2)


def pages_place(got, pages_dev, chips, rows):
    count = 2 * pages_dev
    pieces = got[:, :, :-128].reshape(chips * count, -1)
    marks = got[:, 0, -128:][:, : 2 * count].astype(jnp.int32).reshape(chips * count, 2)
    code = jnp.where(marks[:, 0] < 0, -1, marks[:, 0] * pages_dev + marks[:, 1])
    placing = (code[None, :] == jnp.arange(code.shape[0], dtype=jnp.int32)[:, None]).astype(BF)
    return dot32(placing, pieces).astype(BF).reshape(chips, rows, -1)


def pages_in(got, core, swap, shape):
    pages_dev = shape[0]
    got = got.reshape(got.shape[0], 2 * pages_dev, -1)
    keep, give = by_core(core, (got[:, :pages_dev], got[:, pages_dev:]))
    pair = by_core(core, (keep, lax.ppermute(give, "node", swap)))
    return jnp.stack(pair, axis=1).transpose(2, 0, 1, 3).reshape(shape)


def shards(
    hidden_states,
    norm_gain,
    expert_ids,
    gate_weights,
    w_gate,
    w_up,
    w_down,
    kv_pages,
    page_table,
    kv_lengths,
):
    nodes = lax.axis_size("node")
    experts = nodes // 2
    tok_rows, width = hidden_states.shape
    top = expert_ids.shape[1]
    cap = tok_rows * top * 3 // (2 * experts)

    core = lax.axis_index("node") % 2
    swap = [(i, i ^ 1) for i in range(nodes)]
    pages_dev = kv_pages.shape[0]
    large = cap * 2 // 3
    small = cap - large

    flat = expert_ids.reshape(-1)
    pairs = flat.shape[0]
    onehot = flat[:, None] == jnp.arange(experts, dtype=jnp.int32)[None, :]
    steps = jnp.arange(pairs, dtype=jnp.int32)
    before = dot32((steps[:, None] > steps[None, :]).astype(BF), onehot.astype(BF))
    rank = jnp.sum(jnp.where(onehot, before, 0.0), axis=1).astype(jnp.int32)
    ids = expert_ids[:, :, None]
    rank = rank.reshape(tok_rows, top, 1)
    values = hidden_states.astype(F32)
    factor = lax.rsqrt(jnp.mean(values * values, axis=1, keepdims=True) + 1e-06)
    normed = (values * factor * norm_gain[None, :]).astype(BF)

    parity = [list(range(c, nodes, 2)) for c in (0, 1)]

    def both(w):
        return w[0], lax.ppermute(w, "node", swap)[0]

    weights = list(zip(both(w_gate), both(w_up), both(w_down)))

    def hits(first, count):
        inside = (rank >= first) & (rank < first + count)
        slot = jnp.where(inside, ids * count + rank - first, -1)
        return slot == jnp.arange(experts * count, dtype=jnp.int32)[None, None, :]

    def send(first, count):
        placed = jnp.any(hits(first, count), axis=1).astype(BF)
        rows = lax.dot_general(
            placed, normed, (((0,), (0,)), ((), ())), preferred_element_type=F32
        )
        return rows.astype(BF).reshape(experts, count, width)

    def exchange(x):
        return all_to_all(x, parity)

    def expert(x):
        total = None
        for gate_w, up_w, down_w in weights:
            activated = (jax.nn.silu(dot32(x, gate_w)) * dot32(x, up_w)).astype(BF)
            part = dot32(activated, down_w)
            total = part if total is None else total + part
        return total.astype(BF)

    def combine(first, count, returned):
        scale = jnp.sum(jnp.where(hits(first, count), gate_weights[:, :, None], 0.0), axis=1)
        high = scale.astype(BF)
        low = (scale - high.astype(F32)).astype(BF)
        return dot32(high, returned) + dot32(low, returned)

    one = exchange(send(0, large)).reshape(-1, width)
    pages = pages_out(kv_pages, page_table, kv_lengths, core, swap, experts, small)
    two_out = jnp.concatenate([send(large, small), pages], axis=2)
    two_out, one = lax.optimization_barrier((two_out, one))
    two = exchange(two_out)
    one_done = expert(one).reshape(experts, large, width)
    extra = 2 * kv_pages.size // (nodes * large)
    one_done = lax.optimization_barrier(jnp.pad(one_done, ((0, 0), (0, 0), (0, extra))))
    slots = pages_place(two[:, :, width:], pages_dev, experts, large)
    two = two[:, :, :width].reshape(-1, width)
    one_back = exchange(lax.dynamic_update_slice(one_done, slots, (0, 0, width)))
    two_done = expert(two).reshape(experts, small, width)
    two_done, one_back = lax.optimization_barrier((two_done, one_back))
    two_back = exchange(two_done).reshape(-1, width)
    decode_pages = pages_in(one_back[:, :, width:], core, swap, kv_pages.shape)
    one_back = one_back[:, :, :width].reshape(-1, width)
    moe_output = (combine(0, large, one_back) + combine(large, small, two_back)).astype(BF)
    return (moe_output, decode_pages)


def solution(mesh):
    placed = (
        P(("groups", "node"), None),
        P(),
        P(("groups", "node"), None),
        P(("groups", "node"), None),
        P("node", None, None),
        P("node", None, None),
        P("node", None, None),
        P(("groups", "node"), None, None),
        P(("groups", "node"), None),
        P(("groups", "node")),
    )
    return jax.shard_map(
        shards,
        mesh=mesh,
        in_specs=placed,
        out_specs=(P(("groups", "node"), None), P(("groups", "node"), None, None)),
        check_vma=False,
    )
```

```python
import jax
import jax.numpy as jnp
from jax import lax
from jax.sharding import PartitionSpec as P

BF = jnp.bfloat16
F32 = jnp.float32


def dot32(a, b):
    return jnp.dot(a, b, preferred_element_type=F32)


def all_to_all(x, groups=None):
    return lax.all_to_all(
        x, "node", split_axis=0, concat_axis=0, axis_index_groups=groups, tiled=True
    )


def by_core(core, pair):
    first, second = pair
    return jnp.where(core == 0, first, second), jnp.where(core == 0, second, first)


def pages_out(kv_pages, page_table, kv_lengths, core, swap, chips, rows):
    pages_dev, page_len, kv_width = kv_pages.shape
    live = jnp.arange(pages_dev, dtype=jnp.int32) < kv_lengths[0]
    marks = jnp.stack([jnp.where(live, page_table[:, 0], -1), page_table[:, 1]], axis=1)
    marks = jnp.concatenate([marks, lax.ppermute(marks, "node", swap)], axis=0)
    split = kv_pages.reshape(pages_dev, chips, 2, -1)
    keep, give = by_core(core, (split[:, :, 0], split[:, :, 1]))
    pieces = jnp.concatenate([keep, lax.ppermute(give, "node", swap)], axis=0).swapaxes(0, 1)
    tail = jnp.pad(marks.reshape(-1).astype(BF), (0, 128 - marks.size))
    tail = jnp.broadcast_to(tail[None, None, :], (chips, rows, 128))
    return jnp.concatenate([pieces.reshape(chips, rows, -1), tail], axis=2)


def pages_place(got, pages_dev, chips, rows):
    count = 2 * pages_dev
    pieces = got[:, :, :-128].reshape(chips * count, -1)
    marks = got[:, 0, -128:][:, : 2 * count].astype(jnp.int32).reshape(chips * count, 2)
    code = jnp.where(marks[:, 0] < 0, -1, marks[:, 0] * pages_dev + marks[:, 1])
    placing = (code[None, :] == jnp.arange(code.shape[0], dtype=jnp.int32)[:, None]).astype(BF)
    return dot32(placing, pieces).astype(BF).reshape(chips, rows, -1)


def pages_in(got, core, swap, shape):
    pages_dev = shape[0]
    got = got.reshape(got.shape[0], 2 * pages_dev, -1)
    keep, give = by_core(core, (got[:, :pages_dev], got[:, pages_dev:]))
    pair = by_core(core, (keep, lax.ppermute(give, "node", swap)))
    return jnp.stack(pair, axis=1).transpose(2, 0, 1, 3).reshape(shape)


def shards(
    hidden_states,
    norm_gain,
    expert_ids,
    gate_weights,
    w_gate,
    w_up,
    w_down,
    kv_pages,
    page_table,
    kv_lengths,
):
    nodes = lax.axis_size("node")
    experts = nodes // 2
    tok_rows, width = hidden_states.shape
    top = expert_ids.shape[1]
    cap = tok_rows * top * 3 // (2 * experts)

    core = lax.axis_index("node") % 2
    swap = [(i, i ^ 1) for i in range(nodes)]
    pages_dev = kv_pages.shape[0]
    large = cap * 2 // 3
    small = cap - large

    ids = expert_ids[:, :, None]
    named = ids == jnp.arange(experts, dtype=jnp.int32)[None, None, :]
    steps = jnp.arange(tok_rows, dtype=jnp.int32)
    counts = jnp.sum(named.astype(F32), axis=1).astype(BF)
    before = dot32((steps[:, None] > steps[None, :]).astype(BF), counts)
    rank = jnp.sum(jnp.where(named, before[:, None, :], 0.0), axis=2, keepdims=True).astype(jnp.int32)

    values = hidden_states.astype(F32)
    factor = lax.rsqrt(jnp.mean(values * values, axis=1, keepdims=True) + 1e-06)
    normed = (values * factor * norm_gain[None, :]).astype(BF)

    parity = [list(range(c, nodes, 2)) for c in (0, 1)]

    def both(w):
        return w[0], lax.ppermute(w, "node", swap)[0]

    weights = list(zip(both(w_gate), both(w_up), both(w_down)))

    def hits(first, count):
        inside = (rank >= first) & (rank < first + count)
        slot = jnp.where(inside, ids * count + rank - first, -1)
        return slot == jnp.arange(experts * count, dtype=jnp.int32)[None, None, :]

    def send(first, count):
        placed = jnp.any(hits(first, count), axis=1).astype(BF)
        rows = lax.dot_general(
            placed, normed, (((0,), (0,)), ((), ())), preferred_element_type=F32
        )
        return rows.astype(BF).reshape(experts, count, width)

    def exchange(x):
        return all_to_all(x, parity)

    def expert(x):
        total = None
        for gate_w, up_w, down_w in weights:
            activated = (jax.nn.silu(dot32(x, gate_w)) * dot32(x, up_w)).astype(BF)
            part = dot32(activated, down_w)
            total = part if total is None else total + part
        return total.astype(BF)

    def combine(first, count, returned):
        scale = jnp.sum(jnp.where(hits(first, count), gate_weights[:, :, None], 0.0), axis=1)
        high = scale.astype(BF)
        low = (scale - high.astype(F32)).astype(BF)
        return dot32(high, returned) + dot32(low, returned)

    one = exchange(send(0, large)).reshape(-1, width)
    pages = pages_out(kv_pages, page_table, kv_lengths, core, swap, experts, small)
    two_out = jnp.concatenate([send(large, small), pages], axis=2)
    two_out, one = lax.optimization_barrier((two_out, one))
    two = exchange(two_out)
    one_done = expert(one).reshape(experts, large, width)
    extra = 2 * kv_pages.size // (nodes * large)
    one_done = lax.optimization_barrier(jnp.pad(one_done, ((0, 0), (0, 0), (0, extra))))
    slots = pages_place(two[:, :, width:], pages_dev, experts, large)
    two = two[:, :, :width].reshape(-1, width)
    one_back = exchange(lax.dynamic_update_slice(one_done, slots, (0, 0, width)))
    two_done = expert(two).reshape(experts, small, width)
    two_done, one_back = lax.optimization_barrier((two_done, one_back))
    two_back = exchange(two_done).reshape(-1, width)
    decode_pages = pages_in(one_back[:, :, width:], core, swap, kv_pages.shape)
    one_back = one_back[:, :, :width].reshape(-1, width)
    moe_output = (combine(0, large, one_back) + combine(large, small, two_back)).astype(BF)
    return (moe_output, decode_pages)


def solution(mesh):
    placed = (
        P(("groups", "node"), None),
        P(),
        P(("groups", "node"), None),
        P(("groups", "node"), None),
        P("node", None, None),
        P("node", None, None),
        P("node", None, None),
        P(("groups", "node"), None, None),
        P(("groups", "node"), None),
        P(("groups", "node")),
    )
    return jax.shard_map(
        shards,
        mesh=mesh,
        in_specs=placed,
        out_specs=(P(("groups", "node"), None), P(("groups", "node"), None, None)),
        check_vma=False,
    )
```
